32 devices in a mesh: groups: 2 (over y), gx: 4 (over z), gy: 2 (over x), gz: 2 (over core).
Axes of the slice: x: 2, y: 2, z: 4, core: 2. Of those that a mesh axis runs over, the one named last changes fastest.
Arguments:
- positions: float32 [8, 2, 2, 3, 128], P(('groups', 'gx'), 'gy', 'gz'), parts along dimension 0, may hold values from 0 to 1
- species: int32 [8, 2, 2, 128], P(('groups', 'gx'), 'gy', 'gz'), parts along dimension 0, may hold values from 0 to 9
- atom_count: int32 [8, 2, 2, 1], P(('groups', 'gx'), 'gy', 'gz'), parts along dimension 0, may hold values from 64 to 128, as said below
- boundary: int32 [8, 2, 2, 32], P(('groups', 'gx'), 'gy', 'gz'), parts along dimension 0, may hold values from 0 to 127, as said below
- senders: int32 [8, 2, 2, 32, 128], P(('groups', 'gx'), 'gy', 'gz'), parts along dimension 0, may hold values from 0 to 991, as said below
- neighbour_count: int32 [8, 2, 2, 128], P(('groups', 'gx'), 'gy', 'gz'), parts along dimension 0, may hold values from 8 to 32, as said below
- embed: float32 [10, 128], replicated, may hold values from -6 to 6
- radial_first: float32 [2, 8, 64], replicated, may hold values from -2 to 2
- radial_second: float32 [2, 64, 128], replicated, may hold values from -0.75 to 0.75
- mix: float32 [2, 384, 128], replicated, may hold values from -0.3125 to 0.3125
- readout: float32 [128], replicated, may hold values from -0.5 to 0.5
Outputs:
- forces: float32 [8, 2, 2, 3, 128], P(('groups', 'gx'), 'gy', 'gz'), parts along dimension 0
- energy: float32 [2], P('groups'), parts along dimension 0
The draws below stay inside these ranges and needn't reach their ends.
There are 2 independent parts, one for each index of `groups`. The reference program is written for one: setup_inputs(seed, part) draws one part's arguments, and reference() takes and returns one part's arrays. A program takes and returns all parts, laid end to end along the dimension named above; an argument that names none is the same for every part. Nothing has to cross between parts.
Inputs may be any that keep to these rules, and one draw needn't show every extreme that they name: `atom_count`: one brick in every draw holds 128 live atoms. `boundary`: each entry is below its brick's atom_count. `senders`: an own atom below its brick's atom_count, or 128 + slot * 32 + row with slot not 13. `neighbour_count`: every brick in every draw has an atom with all 32 slots live.
All inputs are finite; a program needn't handle non-finite values.
Results may differ from the reference program's by a relative error of at most 0.000082.
Values sent between devices are 32-bit elements; how exact they have to be, the bound alone decides.
A program may use at most 64 MiB of HBM per device.

```python
import math
import jax
import jax.numpy as jnp
import numpy as np
from jax import lax

C = 128
RH = 64
NB = 8
NSPEC = 10
NEIGH = 32
ATOM_DEV = 128
BOUND = 32
BX = 4
BY = 2
BZ = 2


def live_atoms(key):
    base = jax.random.randint(jax.random.fold_in(key, 11), (BX, BY, BZ, 1), ATOM_DEV // 2, ATOM_DEV + 1)
    chosen = jax.random.randint(jax.random.fold_in(key, 12), (), 0, BX * BY * BZ)
    flat = jnp.arange(BX * BY * BZ, dtype=jnp.int32).reshape(BX, BY, BZ, 1)
    return jnp.where(flat == chosen, ATOM_DEV, base)


def draw_atom_count(key, part):
    return live_atoms(key)


def draw_boundary(key, part):
    live = live_atoms(key)
    key = jax.random.fold_in(key, 3)
    raw = jax.random.randint(key, (BX, BY, BZ, BOUND), 0, 1 << 20)
    return raw % live


def draw_senders(key, part):
    live = live_atoms(key)[:, :, :, :, None]
    key = jax.random.fold_in(key, 5)
    shape = (BX, BY, BZ, NEIGH, ATOM_DEV)
    raw = jax.random.randint(jax.random.fold_in(key, 1), shape, 0, 1 << 20)
    own = raw % live
    face = jax.random.randint(jax.random.fold_in(key, 2), shape, 0, 26)
    slot = face + (face >= 13).astype(jnp.int32)
    row = jax.random.randint(jax.random.fold_in(key, 3), shape, 0, BOUND)
    ghost = ATOM_DEV + slot * BOUND + row
    coin = jax.random.randint(jax.random.fold_in(key, 4), shape, 0, 2)
    return jnp.where(coin == 1, ghost, own)


def draw_neighbour_count(key, part):
    key = jax.random.fold_in(key, 6)
    base = jax.random.randint(jax.random.fold_in(key, 1), (BX, BY, BZ, ATOM_DEV), NEIGH // 4, NEIGH + 1)
    chosen = jax.random.randint(jax.random.fold_in(key, 2), (BX, BY, BZ, 1), 0, ATOM_DEV)
    index = jnp.arange(ATOM_DEV, dtype=jnp.int32).reshape(1, 1, 1, ATOM_DEV)
    return jnp.where(index == chosen, NEIGH, base)


def set_ends(drawn, stream_key, low, top_value):
    index_at = [jax.random.randint(jax.random.fold_in(stream_key, axis), (), 0, length) for axis, length in enumerate(drawn.shape)]
    main_axis = drawn.shape.index(max(drawn.shape))
    next_to = index_at[:main_axis] + [(index_at[main_axis] + 1) % drawn.shape[main_axis]] + index_at[main_axis + 1:]
    return drawn.at[tuple(index_at)].set(low).at[tuple(next_to)].set(top_value)


def shard_levels(stream_key, extent, cuts, smallest, largest):
    level, own = 1.0, jax.random.fold_in(stream_key, 6)
    for axis_at, blocks in cuts:
        heights = jnp.exp(jax.random.uniform(jax.random.fold_in(own, axis_at), (blocks,), jnp.float32, smallest / len(cuts), largest / len(cuts)))
        level = level * jnp.repeat(heights, extent[axis_at] // blocks).reshape([-1 if axis == axis_at else 1 for axis in range(len(extent))])
    return level


def rank_bounds(amount, slope):
    weights = [(1 << 20) // math.isqrt(standing ** slope) + 1 for standing in range(1, amount + 1)]
    scale = 1 + sum(weights) // (1 << 30)
    return np.cumsum(np.array([max(1, weight // scale) for weight in weights]))


def ranked_ids(stream_key, shape, amount, skew):
    listing = rank_bounds(amount, skew)
    ticket = jax.random.randint(jax.random.fold_in(stream_key, 1), shape, 0, int(listing[amount - 1]))
    grade = jnp.searchsorted(jnp.asarray(listing, jnp.int32), ticket, side="right")
    return jax.random.permutation(jax.random.fold_in(stream_key, 2), amount)[grade].astype(jnp.int32)


def noise(key, shape, spread, reach, held_as=jnp.bfloat16):
    array = jax.random.normal(key, shape, jnp.float32) * spread
    return jnp.minimum(jnp.maximum(array, -reach), reach).astype(held_as)


def setup_inputs(seed: int = 0, part: int = 0) -> dict:
    streams_of = jax.random.split(jax.random.key(seed), 12)
    part_splits = jax.random.split(jax.random.fold_in(streams_of[11], part), 12)
    return {
        "positions": jnp.clip(1.0 * jax.random.uniform(part_splits[0], (BX, BY, BZ, 3, ATOM_DEV), jnp.float32) ** shard_levels(part_splits[0], (BX, BY, BZ, 3, ATOM_DEV), ((0, 4), (1, 2), (2, 2)), -0.2, 0.2), 0.0, 1.0),
        "species": set_ends(ranked_ids(part_splits[1], (BX, BY, BZ, ATOM_DEV), NSPEC, 2), jax.random.fold_in(part_splits[1], 3), 0, NSPEC - 1).astype(jnp.int32),
        "atom_count": draw_atom_count(jax.random.fold_in(jax.random.fold_in(streams_of[11], part), 71), part),
        "boundary": draw_boundary(jax.random.fold_in(jax.random.fold_in(streams_of[11], part), 71), part),
        "senders": draw_senders(jax.random.fold_in(jax.random.fold_in(streams_of[11], part), 71), part),
        "neighbour_count": draw_neighbour_count(jax.random.fold_in(jax.random.fold_in(streams_of[11], part), 71), part),
        "embed": noise(streams_of[6], (NSPEC, C), 1.0, 6.0, jnp.float32),
        "radial_first": noise(streams_of[7], (2, NB, RH), NB ** -0.5, 2.0, jnp.float32),
        "radial_second": noise(streams_of[8], (2, RH, C), RH ** -0.5, 0.75, jnp.float32),
        "mix": noise(streams_of[9], (2, 3 * C, C), (3 * C) ** -0.5, 0.3125, jnp.float32),
        "readout": noise(streams_of[10], (C,), C ** -0.5, 0.5, jnp.float32),
    }


SOFTEN = 0.5
CUTOFF = 4.0
NEIGHBOURS = 32.0

def offsets_table():
    grid = jnp.arange(27, dtype=jnp.int32)
    return jnp.stack([grid // 9 - 1, grid // 3 % 3 - 1, grid % 3 - 1], axis=0).astype(jnp.float32)

def harmonics(unit):
    ux, uy, uz = (unit[0], unit[1], unit[2])
    root3 = 3.0 ** 0.5
    root5 = 5.0 ** 0.5
    root15 = 15.0 ** 0.5
    return jnp.stack([jnp.ones_like(ux), root3 * ux, root3 * uy, root3 * uz, root15 * ux * uy, root15 * uy * uz, root15 * uz * ux, 0.5 * root15 * (ux * ux - uy * uy), 0.5 * root5 * (3.0 * uz * uz - 1.0)], axis=0)

def interaction(own_xyz, ghost_xyz, own_feat, ghost_feat, links, live_edges, w_first, w_second, w_mix):
    high = lax.Precision.HIGHEST
    shifted = ghost_xyz + offsets_table().T[:, :, None]
    table_xyz = jnp.concatenate([own_xyz, jnp.transpose(shifted, (1, 0, 2)).reshape(3, -1)], 1)
    table_feat = jnp.concatenate([own_feat, ghost_feat.reshape(-1, own_feat.shape[1])], 0)
    delta = table_xyz[:, links] - own_xyz[:, None, :]
    dist = jnp.sqrt(lax.optimization_barrier(jnp.sum(delta * delta, 0)) + SOFTEN * SOFTEN)
    ylm = harmonics(delta / dist[None])
    order = jnp.arange(1, w_first.shape[0] + 1, dtype=jnp.int32).astype(jnp.float32)
    scaled = dist / CUTOFF
    envelope = (1.0 - scaled * scaled) * (1.0 - scaled * scaled)
    basis = jnp.sin(order[:, None, None] * jnp.pi * scaled[None]) * (envelope / dist)[None]
    hidden = jax.nn.silu(jnp.einsum('bna,bh->nah', basis, w_first, precision=high))
    radial = jnp.einsum('nah,hc->nac', hidden, w_second, precision=high)
    message = radial * table_feat[links] * live_edges[:, :, None]
    density = jnp.einsum('kna,nac->akc', ylm, message, precision=high) / NEIGHBOURS
    invariants = jnp.concatenate([density[:, 0], lax.optimization_barrier(jnp.sum(density[:, 1:4] * density[:, 1:4], 1)), lax.optimization_barrier(jnp.sum(density[:, 4:9] * density[:, 4:9], 1))], 1)
    return own_feat + jax.nn.silu(jnp.dot(invariants, w_mix, precision=high))

def ghosts_of(field):
    pieces = []
    for slot in range(27):
        shift_x, shift_y, shift_z = (slot // 9 - 1, slot // 3 % 3 - 1, slot % 3 - 1)
        pieces.append(jnp.roll(field, (-shift_x, -shift_y, -shift_z), axis=(0, 1, 2)))
    return jnp.stack(pieces, axis=3)

def reference(positions, species, atom_count, boundary, senders, neighbour_count, embed, radial_first, radial_second, mix, readout):
    bricks = BX * BY * BZ
    slot_index = jnp.arange(NEIGH, dtype=jnp.int32)
    edge_live = (slot_index[None, :, None] < neighbour_count.reshape(bricks, 1, ATOM_DEV)).astype(jnp.float32)
    atom_live = (jnp.arange(ATOM_DEV, dtype=jnp.int32)[None, None, None, :] < atom_count).astype(jnp.float32).reshape(bricks, ATOM_DEV)
    links = senders.reshape(bricks, NEIGH, ATOM_DEV)
    start_own = jnp.take(embed, species, axis=0).reshape(bricks, ATOM_DEV, C)
    rim_kinds = jnp.take_along_axis(species, boundary, axis=3)
    start_ghost = jnp.take(embed, ghosts_of(rim_kinds), axis=0).reshape(bricks, 27, BOUND, C)
    rim_index = jnp.broadcast_to(boundary[:, :, :, None, :], (BX, BY, BZ, 3, BOUND))
    feat_index = jnp.broadcast_to(boundary[:, :, :, :, None], (BX, BY, BZ, BOUND, C))

    def first_brick(items):
        return interaction(items[0], items[1], items[2], items[3], items[4], items[5], radial_first[0], radial_second[0], mix[0])

    def second_brick(items):
        final = interaction(items[0], items[1], items[2], items[3], items[4], items[5], radial_first[1], radial_second[1], mix[1])
        return jnp.sum(items[6] * jnp.dot(jax.nn.silu(final), readout, precision=lax.Precision.HIGHEST))

    def total_energy(coords):
        rim_xyz = jnp.take_along_axis(coords, rim_index, axis=4)
        ghost_xyz = ghosts_of(rim_xyz).reshape(bricks, 27, 3, BOUND)
        own_xyz = coords.reshape(bricks, 3, ATOM_DEV)
        hidden = lax.map(jax.checkpoint(first_brick), (own_xyz, ghost_xyz, start_own, start_ghost, links, edge_live))
        rim_hidden = jnp.take_along_axis(hidden.reshape(BX, BY, BZ, ATOM_DEV, C), feat_index, axis=3)
        ghost_hidden = ghosts_of(rim_hidden).reshape(bricks, 27, BOUND, C)
        energies = lax.map(jax.checkpoint(second_brick), (own_xyz, ghost_xyz, hidden, ghost_hidden, links, edge_live, atom_live))
        return jnp.sum(energies)
    total, gradient = jax.value_and_grad(total_energy)(positions)
    return (-gradient, (total / (bricks * ATOM_DEV)).reshape(1))
```

```python
import functools
import itertools

import jax
import jax.numpy as jnp
from jax import lax
from jax.experimental import pallas as pl
from jax.experimental.pallas import tpu as pltpu
from jax.sharding import PartitionSpec as P

AXES = ("gx", "gy", "gz")
ATOMS, CH, NEIGH, RH, NB, RIM, NSPEC = 128, 128, 32, 64, 8, 32, 10
GROUP = 4
STEPS = NEIGH // GROUP
WIDE = GROUP * ATOMS
F32, BF16 = jnp.float32, jnp.bfloat16
NN = (((1,), (0,)), ((), ()))
NT = (((1,), (1,)), ((), ()))
TN = (((0,), (0,)), ((), ()))
R3, R5, R15 = 3.0**0.5, 5.0**0.5, 15.0**0.5
PI = 3.141592653589793


def split2(x):
    hi = x.astype(BF16).astype(F32)
    return hi, x - hi


def split3(x):
    a, rest = split2(x)
    b, c = split2(rest)
    return a, b, c


def mm(a, b, dims):
    return lax.dot_general(a.astype(BF16), b.astype(BF16), dims, preferred_element_type=F32)


def dot3(a, b, dims):
    ah, al = split2(a)
    bh, bl = split2(b)
    return mm(ah, bh, dims) + (mm(ah, bl, dims) + mm(al, bh, dims))


def sigmoid(x):
    return 1.0 / (1.0 + jnp.exp(-x))


def lanes(value, q):
    return value[:, q * ATOMS : (q + 1) * ATOMS]


def plan(sizes):
    counts = [2 if s == 2 else 3 for s in sizes]
    moves = []
    for code in itertools.product(*[range(c) for c in counts]):
        moves.append(tuple({0: 0, 1: 1, 2: s - 1}[c] for c, s in zip(code, sizes)))
    return counts, moves[1:]


def kernel(
    sizes,
    pos_ref, spec_ref, count_ref, bound_ref, send_ref, ncount_ref,
    emb_ref, w1_ref, w2_ref, mix_ref, read_ref,
    force_ref, energy_ref,
    geo, rimgeo, geoland, oh, rid, off, gsc, bsc, dbp, yref, geom,
    pre, rad, feat, msg, dens, inv, dd, dysum, dbsum, dg, dr, ddsc, empad,
    rimh, hland, gland, dtab, gtab, cland, ex, ey, ez, etile,
    geo_s, geo_r, h_s, h_r, g_s, g_r, c_s, c_r, ex_s, ex_r, ey_s, ey_r, ez_s, ez_r,
):
    counts, moves = plan(sizes)
    D = len(moves)
    K = oh.shape[1]
    me = [lax.axis_index(a) for a in AXES]

    def at(move, sign):
        return {
            a: lax.rem(m + (d if sign > 0 else s - d), s)
            for a, m, d, s in zip(AXES, me, move, sizes)
        }

    def remote(src, dst, s_sem, r_sem, where):
        return pltpu.make_async_remote_copy(
            src_ref=src, dst_ref=dst, send_sem=s_sem, recv_sem=r_sem,
            device_id=where, device_id_type=pl.DeviceIdType.MESH,
        )

    spare = hland.shape[0] - D * RIM
    if spare:
        hland[D * RIM :, :] = jnp.zeros((spare, CH), F32)
        gland[D * RIM :, :] = jnp.zeros((spare, CH), F32)

    partners = list(moves)
    for axis, s in enumerate(sizes):
        for d in range(1, s):
            move = tuple(d if i == axis else 0 for i in range(3))
            if move not in partners:
                partners.append(move)
    barrier = pltpu.get_barrier_semaphore()
    for move in partners:
        pl.semaphore_signal(barrier, inc=1, device_id=at(move, 1), device_id_type=pl.DeviceIdType.MESH)

    brow = bound_ref[0, 0]
    brow = jnp.concatenate([brow] * 4, axis=1)
    atom_row = lax.broadcasted_iota(jnp.int32, (ATOMS, ATOMS), 0)
    pick = (atom_row == brow).astype(F32)
    pick_t = pick.T
    coords = pos_ref[0, 0, 0]
    kinds = spec_ref[0, 0].astype(F32)
    geo[...] = jnp.zeros_like(geo)
    geo[0:3, :] = coords
    geo[3:4, :] = kinds
    own_geo = geo[...]
    g0, g1, g2 = split3(own_geo)
    rimgeo[...] = (mm(g0, pick, NN) + mm(g1, pick, NN)) + mm(g2, pick, NN)

    pl.semaphore_wait(barrier, len(partners))
    geo_copies = [
        remote(rimgeo, geoland.at[j], geo_s.at[j], geo_r.at[j], at(moves[j], -1)) for j in range(D)
    ]
    for c in geo_copies:
        c.start()

    s = send_ref[0, 0, 0]
    slot_index = lax.broadcasted_iota(jnp.int32, (NEIGH, ATOMS), 0)
    live = slot_index < ncount_ref[0, 0]
    ghost = s >= ATOMS
    t = jnp.where(ghost, s - ATOMS, 0)
    slot = lax.shift_right_logical(t, 5)
    row = t - slot * RIM
    one = lambda c: jnp.where(c, 1, 0)
    sx = one(slot >= 9) + one(slot >= 18)
    rem = slot - 9 * sx
    sy = one(rem >= 3) + one(rem >= 6)
    sz = rem - 3 * sy
    ident = jnp.zeros_like(s)
    for axis, (v, cnt) in enumerate(zip((sx, sy, sz), counts)):
        code = one(v != 1) if cnt == 2 else jnp.where(v == 0, 2, v - 1)
        ident = ident * cnt + code
        off[axis] = jnp.where(ghost, (v - 1).astype(F32), 0.0)
    rows = jnp.where(ghost, ATOMS + (ident - 1) * RIM + row, s)
    rid[...] = jnp.where(live, rows, -1)

    table_row = lax.broadcasted_iota(jnp.int32, (K, ATOMS), 0)

    def build(i, carry):
        for q in range(GROUP):
            r = rid[pl.ds(i * GROUP + q, 1), :]
            oh[i, :, q * ATOMS : (q + 1) * ATOMS] = jnp.where(table_row == r, 1.0, 0.0).astype(BF16)
        return carry

    lax.fori_loop(0, STEPS, build, 0)

    empad[...] = jnp.zeros_like(empad)
    empad[0:NSPEC, :] = emb_ref[...]
    eh, el = split2(empad[...])
    emb_cat = jnp.concatenate([eh, el], axis=0)
    spec_row = lax.broadcasted_iota(jnp.int32, (32, ATOMS), 0)
    spec_row = jnp.where(spec_row >= 16, spec_row - 16, spec_row).astype(F32)
    h0 = mm(emb_cat, (spec_row == kinds).astype(F32), TN)
    ddsc[...] = jnp.zeros_like(ddsc)
    readout = jnp.broadcast_to(read_ref[...], (ATOMS, CH)).T
    live_atoms = (
        lax.broadcasted_iota(jnp.int32, (CH, ATOMS), 1) < count_ref[0, 0]
    ).astype(F32)

    for c in geo_copies:
        c.wait()
    lane_block = lax.shift_right_logical(lax.broadcasted_iota(jnp.int32, (8, ATOMS), 1), 5)
    tiles = [own_geo]
    for tile in range(K // ATOMS - 1):
        value = jnp.zeros((8, ATOMS), F32)
        for b in range(4):
            if tile * 4 + b < D:
                value = jnp.where(lane_block == b, geoland[tile * 4 + b], value)
        tiles.append(value)
    table_geo = jnp.concatenate(split3(jnp.concatenate(tiles, axis=1)), axis=0).astype(BF16)

    def gather_geo(i, carry):
        x = lax.dot_general(table_geo, oh[i], NN, preferred_element_type=F32)
        x = (x[0:8] + x[8:16]) + x[16:24]
        for q in range(GROUP):
            gsc[i * GROUP + q] = lanes(x, q)
        return carry

    lax.fori_loop(0, STEPS, gather_geo, 0)

    deltas = [(gsc[:, a, :] + off[a]) - coords[a : a + 1, :] for a in range(3)]
    dist = jnp.sqrt(deltas[0] * deltas[0] + deltas[1] * deltas[1] + deltas[2] * deltas[2] + 0.25)
    rinv = 1.0 / dist
    ux, uy, uz = (d * rinv for d in deltas)
    geom[0], geom[1], geom[2], geom[3] = ux, uy, uz, rinv
    ylm = [
        None, R3 * ux, R3 * uy, R3 * uz,
        R15 * ux * uy, R15 * uy * uz, R15 * uz * ux,
        (0.5 * R15) * (ux * ux - uy * uy), (0.5 * R5) * (3.0 * uz * uz - 1.0),
    ]
    for k in range(1, 9):
        yref[k] = ylm[k]
    q4 = dist * 0.25
    inner = 1.0 - q4 * q4
    env = inner * inner * rinv
    denv = -(inner * q4 + env) * rinv
    s1, c1 = jnp.sin(PI * q4), jnp.cos(PI * q4)
    sm, cm, sp, cp = s1, c1, jnp.zeros_like(s1), jnp.ones_like(s1)
    for m in range(NB):
        bsc[:, m, :] = sm * env
        dbp[m] = ((m + 1) * PI * 0.25) * cm * env + sm * denv
        sm, sp = 2.0 * c1 * sm - sp, sm
        cm, cp = 2.0 * c1 * cm - cp, cm
    kind_edge = gsc[:, 3, :]
    rid_kind = jnp.where(live, kind_edge, -1.0)
    geom[4] = rid_kind

    def radial(layer, with_feat):
        w1h, w1l = split2(w1_ref[layer])
        w1c = jnp.concatenate([w1h, w1h, w1l], axis=0).astype(BF16)
        w2h, w2l = split2(w2_ref[layer])
        w2c = jnp.concatenate([w2h, w2h, w2l], axis=0).astype(BF16)

        def step(i, carry):
            b = jnp.concatenate([bsc[i * GROUP + q] for q in range(GROUP)], axis=1)
            bh, bl = split2(b)
            bc = jnp.concatenate([bh, bl, bh], axis=0).astype(BF16)
            p = lax.dot_general(w1c, bc, TN, preferred_element_type=F32)
            pre[layer, i] = p
            hid = p * sigmoid(p)
            hh, hl = split2(hid)
            hc = jnp.concatenate([hh, hl, hh], axis=0).astype(BF16)
            r = lax.dot_general(w2c, hc, TN, preferred_element_type=F32)
            rad[i] = r
            if with_feat:
                for q in range(GROUP):
                    kind = geom[4, pl.ds(i * GROUP + q, 1), :]
                    f = mm(emb_cat, (spec_row == kind).astype(F32), TN)
                    feat[layer, i, :, q * ATOMS : (q + 1) * ATOMS] = f
                    msg[layer, i, :, q * ATOMS : (q + 1) * ATOMS] = f * lanes(r, q)
            return carry

        lax.fori_loop(0, STEPS, step, 0)

    def density(layer):
        def step(cb, carry):
            at_rows = pl.ds(pl.multiple_of(cb * 16, 16), 16)
            acc = [None] * 9
            for n in range(NEIGH):
                lo = (n % GROUP) * ATOMS
                m = msg[layer, n // GROUP, at_rows, lo : lo + ATOMS]
                for k in range(9):
                    term = m if k == 0 else m * yref[k, n : n + 1, :]
                    acc[k] = term if n == 0 else acc[k] + term
            acc = [a * (1.0 / NEIGH) for a in acc]
            for k in range(9):
                dens[k, at_rows, :] = acc[k]
            inv[0, at_rows, :] = acc[0]
            inv[1, at_rows, :] = acc[1] * acc[1] + acc[2] * acc[2] + acc[3] * acc[3]
            sq = acc[4] * acc[4]
            for k in range(5, 9):
                sq = sq + acc[k] * acc[k]
            inv[2, at_rows, :] = sq
            return carry

        lax.fori_loop(0, CH // 16, step, 0)
        z = None
        for part in range(3):
            term = dot3(mix_ref[layer, part * CH : (part + 1) * CH, :], inv[part], TN)
            z = term if z is None else z + term
        return z

    def density_grad(layer, dz):
        for part in range(3):
            d = dot3(mix_ref[layer, part * CH : (part + 1) * CH, :], dz, NN)
            if part == 0:
                dd[0] = d * (1.0 / NEIGH)
            else:
                d = d * (2.0 / NEIGH)
                for k in range(1, 4) if part == 1 else range(4, 9):
                    dd[k] = d * dens[k]

    radial(0, True)
    z1 = density(0)
    sig1 = sigmoid(z1)
    h1 = h0 + z1 * sig1
    dz1 = sig1 * (1.0 + z1 * (1.0 - sig1))
    first = [dens[k] for k in range(1, 9)]
    for k in range(1, 9):
        dd[9 + k] = first[k - 1]

    hh, hl = split2(h1)
    rimh[...] = mm(pick_t[0:RIM], hh, NT) + mm(pick_t[0:RIM], hl, NT)
    h_copies = [
        remote(rimh, hland.at[pl.ds(j * RIM, RIM)], h_s.at[j], h_r.at[j], at(moves[j], -1))
        for j in range(D)
    ]
    for c in h_copies:
        c.start()
    radial(1, False)
    for c in h_copies:
        c.wait()

    parts_t = [h1] + [hland[u * ATOMS : (u + 1) * ATOMS, :].T for u in range(K // ATOMS - 1)]
    table_h = jnp.concatenate(split2(jnp.concatenate(parts_t, axis=1)), axis=0).astype(BF16)

    def gather_h(i, carry):
        x = lax.dot_general(table_h, oh[i], NN, preferred_element_type=F32)
        f = x[0:CH] + x[CH : 2 * CH]
        feat[1, i] = f
        msg[1, i] = f * rad[i]
        return carry

    lax.fori_loop(0, STEPS, gather_h, 0)
    z2 = density(1)
    sig2 = sigmoid(z2)
    final = h1 + z2 * sig2
    sigf = sigmoid(final)
    weight = readout * live_atoms
    contrib = weight * (final * sigf)
    part = contrib[0:8]
    for u in range(1, CH // 8):
        part = part + contrib[u * 8 : (u + 1) * 8]

    def spread(axis, land, s_sem, r_sem, value):
        size = sizes[axis]
        mine = me[axis]
        land[mine] = value
        copies = []
        for d in range(1, size):
            move = tuple(d if i == axis else 0 for i in range(3))
            copies.append(remote(land.at[mine], land.at[mine], s_sem.at[d], r_sem.at[d], at(move, 1)))
        for c in copies:
            c.start()
        return copies

    def gathered(axis, land, copies):
        for c in copies:
            c.wait()
        total = land[0]
        for i in range(1, sizes[axis]):
            total = total + land[i]
        return total

    e_copies = spread(0, ex, ex_s, ex_r, part)

    dfinal = weight * (sigf * (1.0 + final * (1.0 - sigf)))
    density_grad(1, dfinal * (sig2 * (1.0 + z2 * (1.0 - sig2))))

    def back_feat(i, carry):
        for q in range(GROUP):
            cut = slice(q * ATOMS, (q + 1) * ATOMS)
            dm = dd[0]
            for k in range(1, 9):
                dm = dm + yref[k, pl.ds(i * GROUP + q, 1), :] * dd[k]
            gh, gl = split2(dm * rad[i, :, cut])
            dg[i, 0:CH, cut] = gh.astype(BF16)
            dg[i, CH : 2 * CH, cut] = gl.astype(BF16)
            dr[i, :, cut] = dm * feat[1, i, :, cut]
        return carry

    lax.fori_loop(0, STEPS, back_feat, 0)

    dtab[...] = jnp.zeros_like(dtab)

    def scatter_h(i, carry):
        dtab[...] += lax.dot_general(oh[i], dg[i], NT, preferred_element_type=F32)
        return carry

    lax.fori_loop(0, STEPS, scatter_h, 0)
    gtab[...] = dtab[:, 0:CH] + dtab[:, CH : 2 * CH]
    g_copies = [
        remote(
            gtab.at[pl.ds(ATOMS + j * RIM, RIM)], gland.at[pl.ds(j * RIM, RIM)],
            g_s.at[j], g_r.at[j], at(moves[j], 1),
        )
        for j in range(D)
    ]
    for c in g_copies:
        c.start()
    own_dh = gtab[0:ATOMS, :].T

    def back_radial(layer, first_pass):
        w1h, w1l = split2(w1_ref[layer])
        w2h, w2l = split2(w2_ref[layer])
        w2c = jnp.concatenate([w2h, w2h, w2l], axis=1).astype(BF16)

        def step(i, carry):
            v = dr[i]
            vh, vl = split2(v)
            vc = jnp.concatenate([vh, vl, vh], axis=0).astype(BF16)
            dhid = lax.dot_general(w2c, vc, NN, preferred_element_type=F32)
            p = pre[layer, i]
            sg = sigmoid(p)
            dp = dhid * (sg * (1.0 + p * (1.0 - sg)))
            ph, p_lo = split2(dp)
            db = mm(w1h, ph, NN) + (mm(w1h, p_lo, NN) + mm(w1l, ph, NN))
            for q in range(GROUP):
                if first_pass:
                    dbsum[i * GROUP + q] = lanes(db, q)
                else:
                    dbsum[i * GROUP + q] += lanes(db, q)
            return carry

        lax.fori_loop(0, STEPS, step, 0)

    def back_sphere(i, carry):
        for q in range(GROUP):
            cut = slice(q * ATOMS, (q + 1) * ATOMS)
            m = msg[1, i, :, cut]
            for k in range(1, 9):
                dysum[k, pl.ds(i * GROUP + q, 1), :] = jnp.sum(m * dd[k], axis=0, keepdims=True)
        return carry

    lax.fori_loop(0, STEPS, back_sphere, 0)
    back_radial(1, True)
    part = gathered(0, ex, e_copies)
    e_copies = spread(1, ey, ey_s, ey_r, part)

    for c in g_copies:
        c.wait()
    back = gland[0:ATOMS, :]
    for u in range(1, gland.shape[0] // ATOMS):
        back = back + gland[u * ATOMS : (u + 1) * ATOMS, :]
    bh, bl = split2(back.T)
    dh1 = dfinal + own_dh + (mm(bh, pick, NT) + mm(bl, pick, NT))
    for k in range(1, 9):
        dens[k] = dd[9 + k]
    density_grad(0, dh1 * dz1)

    def back_first(i, carry):
        for q in range(GROUP):
            cut = slice(q * ATOMS, (q + 1) * ATOMS)
            m = msg[0, i, :, cut]
            dm = dd[0]
            for k in range(1, 9):
                at_n = pl.ds(i * GROUP + q, 1)
                g = dd[k]
                dm = dm + yref[k, at_n, :] * g
                dysum[k, at_n, :] += jnp.sum(m * g, axis=0, keepdims=True)
            dr[i, :, cut] = dm * feat[0, i, :, cut]
        return carry

    lax.fori_loop(0, STEPS, back_first, 0)
    back_radial(0, False)
    part = gathered(1, ey, e_copies)
    e_copies = spread(2, ez, ez_s, ez_r, part)

    ux, uy, uz, rinv = geom[0], geom[1], geom[2], geom[3]
    dy = [None] + [dysum[k] for k in range(1, 9)]
    gx = R3 * dy[1] + R15 * (uy * dy[4] + uz * dy[6] + ux * dy[7])
    gy = R3 * dy[2] + R15 * (ux * dy[4] + uz * dy[5] - uy * dy[7])
    gz = R3 * dy[3] + R15 * (uy * dy[5] + ux * dy[6]) + (3.0 * R5) * uz * dy[8]
    drad = dbsum[:, 0, :] * dbp[0]
    for m in range(1, NB):
        drad = drad + dbsum[:, m, :] * dbp[m]
    drad = drad - (gx * ux + gy * uy + gz * uz) * rinv
    centre = []
    for a, (g, u) in enumerate(((gx, ux), (gy, uy), (gz, uz))):
        d = jnp.where(live, g * rinv + u * drad, 0.0)
        ddsc[:, a, :] = d
        centre.append(jnp.sum(d, axis=0, keepdims=True))

    def scatter_geo(i, carry):
        d = jnp.concatenate([ddsc[i * GROUP + q] for q in range(GROUP)], axis=1)
        d = jnp.concatenate(split2(d), axis=0).astype(BF16)
        return carry + lax.dot_general(d, oh[i], NT, preferred_element_type=F32)

    dxyz = lax.fori_loop(0, STEPS, scatter_geo, jnp.zeros((16, K), F32))
    dxyz = dxyz[0:8] + dxyz[8:16]
    for u in range(K // ATOMS):
        etile[u] = lanes(dxyz, u)
    c_copies = [
        remote(etile.at[1 + j // 4], cland.at[j], c_s.at[j], c_r.at[j], at(moves[j], 1))
        for j in range(D)
    ]
    for c in c_copies:
        c.start()
    part = gathered(2, ez, e_copies)
    slots = float(ATOMS * sizes[0] * sizes[1] * sizes[2])
    energy_ref[...] = jnp.broadcast_to(jnp.sum(part) / slots, energy_ref.shape)
    for c in c_copies:
        c.wait()
    ret = jnp.zeros((8, ATOMS), F32)
    for j in range(D):
        ret = ret + jnp.where(lane_block == j % 4, cland[j], 0.0)
    r0, r1 = split2(ret)
    grad = etile[0] + (mm(r0, pick, NT) + mm(r1, pick, NT))
    for a in range(3):
        force_ref[0, 0, 0, a : a + 1, :] = centre[a] - grad[a : a + 1, :]


def on_device(
    sizes, positions, species, atom_count, boundary, senders, neighbour_count,
    embed, radial_first, radial_second, mix, readout,
):
    _, moves = plan(sizes)
    D = len(moves)
    T = -(-D * RIM // ATOMS)
    K = ATOMS * (1 + T)
    vm = pltpu.VMEM
    dma = pltpu.SemaphoreType.DMA
    scratch = [
        vm((8, ATOMS), F32),
        vm((8, ATOMS), F32),
        vm((D, 8, ATOMS), F32),
        vm((STEPS, K, WIDE), BF16),
        vm((NEIGH, ATOMS), jnp.int32),
        vm((3, NEIGH, ATOMS), F32),
        vm((NEIGH, 8, ATOMS), F32),
        vm((NEIGH, NB, ATOMS), F32),
        vm((NB, NEIGH, ATOMS), F32),
        vm((9, NEIGH, ATOMS), F32),
        vm((5, NEIGH, ATOMS), F32),
        vm((2, STEPS, RH, WIDE), F32),
        vm((STEPS, CH, WIDE), F32),
        vm((2, STEPS, CH, WIDE), F32),
        vm((2, STEPS, CH, WIDE), F32),
        vm((9, CH, ATOMS), F32),
        vm((3, CH, ATOMS), F32),
        vm((18, CH, ATOMS), F32),
        vm((9, NEIGH, ATOMS), F32),
        vm((NEIGH, NB, ATOMS), F32),
        vm((STEPS, 2 * CH, WIDE), BF16),
        vm((STEPS, CH, WIDE), F32),
        vm((NEIGH, 8, ATOMS), F32),
        vm((16, CH), F32),
        vm((RIM, CH), F32),
        vm((T * ATOMS, CH), F32),
        vm((T * ATOMS, CH), F32),
        vm((K, 2 * CH), F32),
        vm((K, CH), F32),
        vm((D, 8, ATOMS), F32),
        vm((sizes[0], 8, ATOMS), F32),
        vm((sizes[1], 8, ATOMS), F32),
        vm((sizes[2], 8, ATOMS), F32),
        vm((1 + T, 8, ATOMS), F32),
    ]
    for amount in (D, D, D, D, sizes[0], sizes[1], sizes[2]):
        scratch += [dma((amount,)), dma((amount,))]
    forces, energy = pl.pallas_call(
        functools.partial(kernel, sizes),
        out_shape=(
            jax.ShapeDtypeStruct((1, 1, 1, 3, ATOMS), F32),
            jax.ShapeDtypeStruct((1, ATOMS), F32),
        ),
        in_specs=[pl.BlockSpec(memory_space=pltpu.VMEM)] * 11,
        out_specs=(pl.BlockSpec(memory_space=pltpu.VMEM),) * 2,
        scratch_shapes=scratch,
        compiler_params=pltpu.CompilerParams(
            collective_id=0, has_side_effects=True, vmem_limit_bytes=50 * 1024 * 1024
        ),
        name="brick",
    )(
        positions, species.reshape(1, 1, 1, ATOMS), atom_count.reshape(1, 1, 1, 1),
        boundary.reshape(1, 1, 1, RIM), senders, neighbour_count.reshape(1, 1, 1, ATOMS),
        embed, radial_first, radial_second, mix, readout.reshape(1, CH),
    )
    return forces, energy[0, 0:1]


def solution(mesh):
    sizes = tuple(mesh.shape[a] for a in AXES)
    brick = lambda extra: P(("groups", "gx"), "gy", "gz", *([None] * extra))
    in_specs = (brick(2), brick(1), brick(1), brick(1), brick(2), brick(1), P(), P(), P(), P(), P())
    return jax.shard_map(
        functools.partial(on_device, sizes),
        mesh=mesh,
        in_specs=in_specs,
        out_specs=(brick(2), P("groups")),
        check_vma=False,
    )
```

```python
import functools
import itertools

import jax
import jax.numpy as jnp
from jax import lax
from jax.experimental import pallas as pl
from jax.experimental.pallas import tpu as pltpu
from jax.sharding import PartitionSpec as P

AXES = ("gx", "gy", "gz")
ATOMS, CH, NEIGH, RH, NB, RIM, NSPEC = 128, 128, 32, 64, 8, 32, 10
GROUP = 4
STEPS = NEIGH // GROUP
WIDE = GROUP * ATOMS
F32, BF16 = jnp.float32, jnp.bfloat16
NN = (((1,), (0,)), ((), ()))
NT = (((1,), (1,)), ((), ()))
TN = (((0,), (0,)), ((), ()))
R3, R5, R15 = 3.0**0.5, 5.0**0.5, 15.0**0.5
PI = 3.141592653589793


def split2(x):
    hi = x.astype(BF16).astype(F32)
    return hi, x - hi


def split3(x):
    a, rest = split2(x)
    b, c = split2(rest)
    return a, b, c


def mm(a, b, dims):
    return lax.dot_general(a.astype(BF16), b.astype(BF16), dims, preferred_element_type=F32)


def dot3(a, b, dims):
    ah, al = split2(a)
    bh, bl = split2(b)
    return mm(ah, bh, dims) + (mm(ah, bl, dims) + mm(al, bh, dims))


def sigmoid(x):
    return 1.0 / (1.0 + jnp.exp(-x))


def lanes(value, q):
    return value[:, q * ATOMS : (q + 1) * ATOMS]


def plan(sizes):
    counts = [2 if s == 2 else 3 for s in sizes]
    moves = []
    for code in itertools.product(*[range(c) for c in counts]):
        moves.append(tuple({0: 0, 1: 1, 2: s - 1}[c] for c, s in zip(code, sizes)))
    return counts, moves[:0:-1]


def kernel(
    sizes,
    pos_any, spec_any, count_any, bound_any, send_any, ncount_any,
    emb_any, w1_any, w2_any, mix_any, read_any,
    force_ref, energy_ref,
    geo, rimgeo, geoland, oh, rid, off, gsc, bsc, dbp, yref, geom,
    pre, rad, feat, msg, dens, inv, dd, dysum, dbsum, dg, dr, ddsc, empad,
    rimh, hland, gland, dtab, gtab, cland, ex, ey, ez, etile,
    pos_ref, spec_ref, count_ref, bound_ref, send_ref, ncount_ref,
    emb_ref, w1_ref, w2_ref, mix_ref, read_ref, in_s,
    geo_s, geo_r, h_s, h_r, g_s, g_r, c_s, c_r, ex_s, ex_r, ey_s, ey_r, ez_s, ez_r,
):
    counts, moves = plan(sizes)
    D = len(moves)
    K = oh.shape[1]
    loads = {}
    for index, (name, src, dst) in enumerate((
        ("bound", bound_any, bound_ref), ("pos", pos_any, pos_ref), ("spec", spec_any, spec_ref),
        ("send", send_any, send_ref), ("ncount", ncount_any, ncount_ref), ("count", count_any, count_ref),
        ("emb", emb_any, emb_ref), ("w1", w1_any, w1_ref), ("w2", w2_any, w2_ref),
        ("read", read_any, read_ref), ("mix", mix_any, mix_ref),
    )):
        loads[name] = pltpu.make_async_copy(src, dst, in_s.at[index])
        loads[name].start()
    me = [lax.axis_index(a) for a in AXES]

    def at(move, sign):
        return {
            a: lax.rem(m + (d if sign > 0 else s - d), s)
            for a, m, d, s in zip(AXES, me, move, sizes)
        }

    def remote(src, dst, s_sem, r_sem, where):
        return pltpu.make_async_remote_copy(
            src_ref=src, dst_ref=dst, send_sem=s_sem, recv_sem=r_sem,
            device_id=where, device_id_type=pl.DeviceIdType.MESH,
        )

    spare = hland.shape[0] - D * RIM
    if spare:
        hland[D * RIM :, :] = jnp.zeros((spare, CH), F32)
        gland[D * RIM :, :] = jnp.zeros((spare, CH), F32)

    partners = list(moves)
    for axis, s in enumerate(sizes):
        for d in range(1, s):
            move = tuple(d if i == axis else 0 for i in range(3))
            if move not in partners:
                partners.append(move)
    barrier = pltpu.get_barrier_semaphore()
    for move in partners:
        pl.semaphore_signal(barrier, inc=1, device_id=at(move, 1), device_id_type=pl.DeviceIdType.MESH)

    for name in ("bound", "pos", "spec"):
        loads[name].wait()
    brow = bound_ref[0, 0]
    brow = jnp.concatenate([brow] * 4, axis=1)
    atom_row = lax.broadcasted_iota(jnp.int32, (ATOMS, ATOMS), 0)
    pick = (atom_row == brow).astype(F32)
    pick_t = pick.T
    coords = pos_ref[0, 0, 0]
    kinds = spec_ref[0, 0].astype(F32)
    geo[...] = jnp.zeros_like(geo)
    geo[0:3, :] = coords
    geo[3:4, :] = kinds
    own_geo = geo[...]
    g0, g1, g2 = split3(own_geo)
    rimgeo[...] = (mm(g0, pick, NN) + mm(g1, pick, NN)) + mm(g2, pick, NN)

    pl.semaphore_wait(barrier, len(partners))
    geo_copies = [
        remote(rimgeo, geoland.at[j], geo_s.at[j], geo_r.at[j], at(moves[j], -1)) for j in range(D)
    ]
    for c in geo_copies:
        c.start()

    for name in ("send", "ncount"):
        loads[name].wait()
    s = send_ref[0, 0, 0]
    slot_index = lax.broadcasted_iota(jnp.int32, (NEIGH, ATOMS), 0)
    live = slot_index < ncount_ref[0, 0]
    ghost = s >= ATOMS
    t = jnp.where(ghost, s - ATOMS, 0)
    slot = lax.shift_right_logical(t, 5)
    row = t - slot * RIM
    one = lambda c: jnp.where(c, 1, 0)
    sx = one(slot >= 9) + one(slot >= 18)
    rem = slot - 9 * sx
    sy = one(rem >= 3) + one(rem >= 6)
    sz = rem - 3 * sy
    ident = jnp.zeros_like(s)
    for axis, (v, cnt) in enumerate(zip((sx, sy, sz), counts)):
        code = one(v != 1) if cnt == 2 else jnp.where(v == 0, 2, v - 1)
        ident = ident * cnt + code
        off[axis] = jnp.where(ghost, (v - 1).astype(F32), 0.0)
    rows = jnp.where(ghost, ATOMS + (D - ident) * RIM + row, s)
    rid[...] = jnp.where(live, rows, -1)

    table_row = lax.broadcasted_iota(jnp.int32, (K, ATOMS), 0)

    def build(i, carry):
        for q in range(GROUP):
            r = rid[pl.ds(i * GROUP + q, 1), :]
            oh[i, :, q * ATOMS : (q + 1) * ATOMS] = jnp.where(table_row == r, 1.0, 0.0).astype(BF16)
        return carry

    lax.fori_loop(0, STEPS, build, 0)

    for name in ("emb", "w1", "w2", "count", "read", "mix"):
        loads[name].wait()
    empad[...] = jnp.zeros_like(empad)
    empad[0:NSPEC, :] = emb_ref[...]
    eh, el = split2(empad[...])
    emb_cat = jnp.concatenate([eh, el], axis=0)
    spec_row = lax.broadcasted_iota(jnp.int32, (32, ATOMS), 0)
    spec_row = jnp.where(spec_row >= 16, spec_row - 16, spec_row).astype(F32)
    h0 = mm(emb_cat, (spec_row == kinds).astype(F32), TN)
    ddsc[...] = jnp.zeros_like(ddsc)
    readout = jnp.broadcast_to(read_ref[...], (ATOMS, CH)).T
    live_atoms = (
        lax.broadcasted_iota(jnp.int32, (CH, ATOMS), 1) < count_ref[0, 0]
    ).astype(F32)

    for c in geo_copies:
        c.wait()
    lane_block = lax.shift_right_logical(lax.broadcasted_iota(jnp.int32, (8, ATOMS), 1), 5)
    tiles = [own_geo]
    for tile in range(K // ATOMS - 1):
        value = jnp.zeros((8, ATOMS), F32)
        for b in range(4):
            if tile * 4 + b < D:
                value = jnp.where(lane_block == b, geoland[tile * 4 + b], value)
        tiles.append(value)
    table_geo = jnp.concatenate(split3(jnp.concatenate(tiles, axis=1)), axis=0).astype(BF16)

    def gather_geo(i, carry):
        x = lax.dot_general(table_geo, oh[i], NN, preferred_element_type=F32)
        x = (x[0:8] + x[8:16]) + x[16:24]
        for q in range(GROUP):
            gsc[i * GROUP + q] = lanes(x, q)
        return carry

    lax.fori_loop(0, STEPS, gather_geo, 0)

    deltas = [(gsc[:, a, :] + off[a]) - coords[a : a + 1, :] for a in range(3)]
    dist = jnp.sqrt(deltas[0] * deltas[0] + deltas[1] * deltas[1] + deltas[2] * deltas[2] + 0.25)
    rinv = 1.0 / dist
    ux, uy, uz = (d * rinv for d in deltas)
    geom[0], geom[1], geom[2], geom[3] = ux, uy, uz, rinv
    ylm = [
        None, R3 * ux, R3 * uy, R3 * uz,
        R15 * ux * uy, R15 * uy * uz, R15 * uz * ux,
        (0.5 * R15) * (ux * ux - uy * uy), (0.5 * R5) * (3.0 * uz * uz - 1.0),
    ]
    for k in range(1, 9):
        yref[k] = ylm[k]
    q4 = dist * 0.25
    inner = 1.0 - q4 * q4
    env = inner * inner * rinv
    denv = -(inner * q4 + env) * rinv
    s1, c1 = jnp.sin(PI * q4), jnp.cos(PI * q4)
    sm, cm, sp, cp = s1, c1, jnp.zeros_like(s1), jnp.ones_like(s1)
    for m in range(NB):
        bsc[:, m, :] = sm * env
        dbp[m] = ((m + 1) * PI * 0.25) * cm * env + sm * denv
        sm, sp = 2.0 * c1 * sm - sp, sm
        cm, cp = 2.0 * c1 * cm - cp, cm
    kind_edge = gsc[:, 3, :]
    rid_kind = jnp.where(live, kind_edge, -1.0)
    geom[4] = rid_kind

    def radial(layer, with_feat):
        w1h, w1l = split2(w1_ref[layer])
        w1c = jnp.concatenate([w1h, w1h, w1l], axis=0).astype(BF16)
        w2h, w2l = split2(w2_ref[layer])
        w2c = jnp.concatenate([w2h, w2h, w2l], axis=0).astype(BF16)

        def step(i, carry):
            b = jnp.concatenate([bsc[i * GROUP + q] for q in range(GROUP)], axis=1)
            bh, bl = split2(b)
            bc = jnp.concatenate([bh, bl, bh], axis=0).astype(BF16)
            p = lax.dot_general(w1c, bc, TN, preferred_element_type=F32)
            pre[layer, i] = p
            hid = p * sigmoid(p)
            hh, hl = split2(hid)
            hc = jnp.concatenate([hh, hl, hh], axis=0).astype(BF16)
            r = lax.dot_general(w2c, hc, TN, preferred_element_type=F32)
            rad[i] = r
            if with_feat:
                for q in range(GROUP):
                    kind = geom[4, pl.ds(i * GROUP + q, 1), :]
                    f = mm(emb_cat, (spec_row == kind).astype(F32), TN)
                    feat[layer, i, :, q * ATOMS : (q + 1) * ATOMS] = f
                    msg[layer, i, :, q * ATOMS : (q + 1) * ATOMS] = f * lanes(r, q)
            return carry

        lax.fori_loop(0, STEPS, step, 0)

    def density(layer):
        def step(cb, carry):
            at_rows = pl.ds(pl.multiple_of(cb * 16, 16), 16)
            acc = [None] * 9
            for n in range(NEIGH):
                lo = (n % GROUP) * ATOMS
                m = msg[layer, n // GROUP, at_rows, lo : lo + ATOMS]
                for k in range(9):
                    term = m if k == 0 else m * yref[k, n : n + 1, :]
                    acc[k] = term if n == 0 else acc[k] + term
            acc = [a * (1.0 / NEIGH) for a in acc]
            for k in range(9):
                dens[k, at_rows, :] = acc[k]
            inv[0, at_rows, :] = acc[0]
            inv[1, at_rows, :] = acc[1] * acc[1] + acc[2] * acc[2] + acc[3] * acc[3]
            sq = acc[4] * acc[4]
            for k in range(5, 9):
                sq = sq + acc[k] * acc[k]
            inv[2, at_rows, :] = sq
            return carry

        lax.fori_loop(0, CH // 16, step, 0)
        z = None
        for part in range(3):
            term = dot3(mix_ref[layer, part * CH : (part + 1) * CH, :], inv[part], TN)
            z = term if z is None else z + term
        return z

    def density_grad(layer, dz):
        for part in range(3):
            d = dot3(mix_ref[layer, part * CH : (part + 1) * CH, :], dz, NN)
            if part == 0:
                dd[0] = d * (1.0 / NEIGH)
            else:
                d = d * (2.0 / NEIGH)
                for k in range(1, 4) if part == 1 else range(4, 9):
                    dd[k] = d * dens[k]

    radial(0, True)
    z1 = density(0)
    sig1 = sigmoid(z1)
    h1 = h0 + z1 * sig1
    dz1 = sig1 * (1.0 + z1 * (1.0 - sig1))
    first = [dens[k] for k in range(1, 9)]
    for k in range(1, 9):
        dd[9 + k] = first[k - 1]

    hh, hl = split2(h1)
    rimh[...] = mm(pick_t[0:RIM], hh, NT) + mm(pick_t[0:RIM], hl, NT)
    h_copies = [
        remote(rimh, hland.at[pl.ds(j * RIM, RIM)], h_s.at[j], h_r.at[j], at(moves[j], -1))
        for j in range(D)
    ]
    for c in h_copies:
        c.start()
    radial(1, False)
    for c in h_copies:
        c.wait()

    parts_t = [h1] + [hland[u * ATOMS : (u + 1) * ATOMS, :].T for u in range(K // ATOMS - 1)]
    table_h = jnp.concatenate(split2(jnp.concatenate(parts_t, axis=1)), axis=0).astype(BF16)

    def gather_h(i, carry):
        x = lax.dot_general(table_h, oh[i], NN, preferred_element_type=F32)
        f = x[0:CH] + x[CH : 2 * CH]
        feat[1, i] = f
        msg[1, i] = f * rad[i]
        return carry

    lax.fori_loop(0, STEPS, gather_h, 0)
    z2 = density(1)
    sig2 = sigmoid(z2)
    final = h1 + z2 * sig2
    sigf = sigmoid(final)
    weight = readout * live_atoms
    contrib = weight * (final * sigf)
    part = contrib[0:8]
    for u in range(1, CH // 8):
        part = part + contrib[u * 8 : (u + 1) * 8]

    def spread(axis, land, s_sem, r_sem, value):
        size = sizes[axis]
        mine = me[axis]
        land[mine] = value
        copies = []
        for d in range(1, size):
            move = tuple(d if i == axis else 0 for i in range(3))
            copies.append(remote(land.at[mine], land.at[mine], s_sem.at[d], r_sem.at[d], at(move, 1)))
        for c in copies:
            c.start()
        return copies

    def gathered(axis, land, copies):
        for c in copies:
            c.wait()
        total = land[0]
        for i in range(1, sizes[axis]):
            total = total + land[i]
        return total

    e_copies = spread(0, ex, ex_s, ex_r, part)

    dfinal = weight * (sigf * (1.0 + final * (1.0 - sigf)))
    density_grad(1, dfinal * (sig2 * (1.0 + z2 * (1.0 - sig2))))

    def back_feat(i, carry):
        for q in range(GROUP):
            cut = slice(q * ATOMS, (q + 1) * ATOMS)
            dm = dd[0]
            for k in range(1, 9):
                dm = dm + yref[k, pl.ds(i * GROUP + q, 1), :] * dd[k]
            gh, gl = split2(dm * rad[i, :, cut])
            dg[i, 0:CH, cut] = gh.astype(BF16)
            dg[i, CH : 2 * CH, cut] = gl.astype(BF16)
            dr[i, :, cut] = dm * feat[1, i, :, cut]
        return carry

    lax.fori_loop(0, STEPS, back_feat, 0)

    dtab[...] = jnp.zeros_like(dtab)

    def scatter_h(i, carry):
        dtab[...] += lax.dot_general(oh[i], dg[i], NT, preferred_element_type=F32)
        return carry

    lax.fori_loop(0, STEPS, scatter_h, 0)
    gtab[...] = dtab[:, 0:CH] + dtab[:, CH : 2 * CH]
    g_copies = [
        remote(
            gtab.at[pl.ds(ATOMS + j * RIM, RIM)], gland.at[pl.ds(j * RIM, RIM)],
            g_s.at[j], g_r.at[j], at(moves[j], 1),
        )
        for j in range(D)
    ]
    for c in g_copies:
        c.start()
    own_dh = gtab[0:ATOMS, :].T

    def back_radial(layer, first_pass):
        w1h, w1l = split2(w1_ref[layer])
        w2h, w2l = split2(w2_ref[layer])
        w2c = jnp.concatenate([w2h, w2h, w2l], axis=1).astype(BF16)

        def step(i, carry):
            v = dr[i]
            vh, vl = split2(v)
            vc = jnp.concatenate([vh, vl, vh], axis=0).astype(BF16)
            dhid = lax.dot_general(w2c, vc, NN, preferred_element_type=F32)
            p = pre[layer, i]
            sg = sigmoid(p)
            dp = dhid * (sg * (1.0 + p * (1.0 - sg)))
            ph, p_lo = split2(dp)
            db = mm(w1h, ph, NN) + (mm(w1h, p_lo, NN) + mm(w1l, ph, NN))
            for q in range(GROUP):
                if first_pass:
                    dbsum[i * GROUP + q] = lanes(db, q)
                else:
                    dbsum[i * GROUP + q] += lanes(db, q)
            return carry

        lax.fori_loop(0, STEPS, step, 0)

    def back_sphere(i, carry):
        for q in range(GROUP):
            cut = slice(q * ATOMS, (q + 1) * ATOMS)
            m = msg[1, i, :, cut]
            for k in range(1, 9):
                dysum[k, pl.ds(i * GROUP + q, 1), :] = jnp.sum(m * dd[k], axis=0, keepdims=True)
        return carry

    lax.fori_loop(0, STEPS, back_sphere, 0)
    back_radial(1, True)
    part = gathered(0, ex, e_copies)
    e_copies = spread(1, ey, ey_s, ey_r, part)

    for c in g_copies:
        c.wait()
    back = gland[0:ATOMS, :]
    for u in range(1, gland.shape[0] // ATOMS):
        back = back + gland[u * ATOMS : (u + 1) * ATOMS, :]
    bh, bl = split2(back.T)
    dh1 = dfinal + own_dh + (mm(bh, pick, NT) + mm(bl, pick, NT))
    for k in range(1, 9):
        dens[k] = dd[9 + k]
    density_grad(0, dh1 * dz1)

    def back_first(i, carry):
        for q in range(GROUP):
            cut = slice(q * ATOMS, (q + 1) * ATOMS)
            m = msg[0, i, :, cut]
            dm = dd[0]
            for k in range(1, 9):
                at_n = pl.ds(i * GROUP + q, 1)
                g = dd[k]
                dm = dm + yref[k, at_n, :] * g
                dysum[k, at_n, :] += jnp.sum(m * g, axis=0, keepdims=True)
            dr[i, :, cut] = dm * feat[0, i, :, cut]
        return carry

    lax.fori_loop(0, STEPS, back_first, 0)
    back_radial(0, False)
    part = gathered(1, ey, e_copies)
    e_copies = spread(2, ez, ez_s, ez_r, part)

    ux, uy, uz, rinv = geom[0], geom[1], geom[2], geom[3]
    dy = [None] + [dysum[k] for k in range(1, 9)]
    gx = R3 * dy[1] + R15 * (uy * dy[4] + uz * dy[6] + ux * dy[7])
    gy = R3 * dy[2] + R15 * (ux * dy[4] + uz * dy[5] - uy * dy[7])
    gz = R3 * dy[3] + R15 * (uy * dy[5] + ux * dy[6]) + (3.0 * R5) * uz * dy[8]
    drad = dbsum[:, 0, :] * dbp[0]
    for m in range(1, NB):
        drad = drad + dbsum[:, m, :] * dbp[m]
    drad = drad - (gx * ux + gy * uy + gz * uz) * rinv
    centre = []
    for a, (g, u) in enumerate(((gx, ux), (gy, uy), (gz, uz))):
        d = jnp.where(live, g * rinv + u * drad, 0.0)
        ddsc[:, a, :] = d
        centre.append(jnp.sum(d, axis=0, keepdims=True))

    def scatter_geo(i, carry):
        d = jnp.concatenate([ddsc[i * GROUP + q] for q in range(GROUP)], axis=1)
        d = jnp.concatenate(split2(d), axis=0).astype(BF16)
        return carry + lax.dot_general(d, oh[i], NT, preferred_element_type=F32)

    dxyz = lax.fori_loop(0, STEPS, scatter_geo, jnp.zeros((16, K), F32))
    dxyz = dxyz[0:8] + dxyz[8:16]
    for u in range(K // ATOMS):
        etile[u] = lanes(dxyz, u)
    c_copies = [
        remote(etile.at[1 + j // 4], cland.at[j], c_s.at[j], c_r.at[j], at(moves[j], 1))
        for j in range(D)
    ]
    for c in c_copies:
        c.start()
    part = gathered(2, ez, e_copies)
    slots = float(ATOMS * sizes[0] * sizes[1] * sizes[2])
    energy_ref[...] = jnp.broadcast_to(jnp.sum(part) / slots, energy_ref.shape)
    for c in c_copies:
        c.wait()
    ret = jnp.zeros((8, ATOMS), F32)
    for j in range(D):
        ret = ret + jnp.where(lane_block == j % 4, cland[j], 0.0)
    r0, r1 = split2(ret)
    grad = etile[0] + (mm(r0, pick, NT) + mm(r1, pick, NT))
    for a in range(3):
        force_ref[0, 0, 0, a : a + 1, :] = centre[a] - grad[a : a + 1, :]


def on_device(
    sizes, positions, species, atom_count, boundary, senders, neighbour_count,
    embed, radial_first, radial_second, mix, readout,
):
    _, moves = plan(sizes)
    D = len(moves)
    T = -(-D * RIM // ATOMS)
    K = ATOMS * (1 + T)
    vm = pltpu.VMEM
    dma = pltpu.SemaphoreType.DMA
    scratch = [
        vm((8, ATOMS), F32),
        vm((8, ATOMS), F32),
        vm((D, 8, ATOMS), F32),
        vm((STEPS, K, WIDE), BF16),
        vm((NEIGH, ATOMS), jnp.int32),
        vm((3, NEIGH, ATOMS), F32),
        vm((NEIGH, 8, ATOMS), F32),
        vm((NEIGH, NB, ATOMS), F32),
        vm((NB, NEIGH, ATOMS), F32),
        vm((9, NEIGH, ATOMS), F32),
        vm((5, NEIGH, ATOMS), F32),
        vm((2, STEPS, RH, WIDE), F32),
        vm((STEPS, CH, WIDE), F32),
        vm((2, STEPS, CH, WIDE), F32),
        vm((2, STEPS, CH, WIDE), F32),
        vm((9, CH, ATOMS), F32),
        vm((3, CH, ATOMS), F32),
        vm((18, CH, ATOMS), F32),
        vm((9, NEIGH, ATOMS), F32),
        vm((NEIGH, NB, ATOMS), F32),
        vm((STEPS, 2 * CH, WIDE), BF16),
        vm((STEPS, CH, WIDE), F32),
        vm((NEIGH, 8, ATOMS), F32),
        vm((16, CH), F32),
        vm((RIM, CH), F32),
        vm((T * ATOMS, CH), F32),
        vm((T * ATOMS, CH), F32),
        vm((K, 2 * CH), F32),
        vm((K, CH), F32),
        vm((D, 8, ATOMS), F32),
        vm((sizes[0], 8, ATOMS), F32),
        vm((sizes[1], 8, ATOMS), F32),
        vm((sizes[2], 8, ATOMS), F32),
        vm((1 + T, 8, ATOMS), F32),
    ]
    operands = (
        positions, species.reshape(1, 1, 1, ATOMS), atom_count.reshape(1, 1, 1, 1),
        boundary.reshape(1, 1, 1, RIM), senders, neighbour_count.reshape(1, 1, 1, ATOMS),
        embed, radial_first, radial_second, mix, readout.reshape(1, CH),
    )
    scratch += [vm(x.shape, x.dtype) for x in operands] + [dma((len(operands),))]
    for amount in (D, D, D, D, sizes[0], sizes[1], sizes[2]):
        scratch += [dma((amount,)), dma((amount,))]
    forces, energy = pl.pallas_call(
        functools.partial(kernel, sizes),
        out_shape=(
            jax.ShapeDtypeStruct((1, 1, 1, 3, ATOMS), F32),
            jax.ShapeDtypeStruct((1, ATOMS), F32),
        ),
        in_specs=[pl.BlockSpec(memory_space=pltpu.HBM)] * 11,
        out_specs=(pl.BlockSpec(memory_space=pltpu.VMEM),) * 2,
        scratch_shapes=scratch,
        compiler_params=pltpu.CompilerParams(
            collective_id=0, has_side_effects=True, vmem_limit_bytes=50 * 1024 * 1024
        ),
        name="brick",
    )(*operands)
    return forces, energy[0, 0:1]


def solution(mesh):
    sizes = tuple(mesh.shape[a] for a in AXES)
    brick = lambda extra: P(("groups", "gx"), "gy", "gz", *([None] * extra))
    in_specs = (brick(2), brick(1), brick(1), brick(1), brick(2), brick(1), P(), P(), P(), P(), P())
    return jax.shard_map(
        functools.partial(on_device, sizes),
        mesh=mesh,
        in_specs=in_specs,
        out_specs=(brick(2), P("groups")),
        check_vma=False,
    )
```

```python
import functools
import itertools

import jax
import jax.numpy as jnp
from jax import lax
from jax.experimental import pallas as pl
from jax.experimental.pallas import tpu as pltpu
from jax.sharding import PartitionSpec as P

AXES = ("gx", "gy", "gz")
ATOMS, CH, NEIGH, RH, NB, RIM, NSPEC = 128, 128, 32, 64, 8, 32, 10
GROUP = 4
STEPS = NEIGH // GROUP
WIDE = GROUP * ATOMS
VMEM_BYTES = 64 * 1024 * 1024
UNROLL = 4
F32, BF16 = jnp.float32, jnp.bfloat16
NN = (((1,), (0,)), ((), ()))
NT = (((1,), (1,)), ((), ()))
TN = (((0,), (0,)), ((), ()))
R3, R5, R15 = 3.0**0.5, 5.0**0.5, 15.0**0.5
PI = 3.141592653589793


def split2(x):
    hi = x.astype(BF16).astype(F32)
    return hi, x - hi


def split3(x):
    a, rest = split2(x)
    b, c = split2(rest)
    return a, b, c


def mm(a, b, dims):
    return lax.dot_general(a.astype(BF16), b.astype(BF16), dims, preferred_element_type=F32)


def dot3(a, b, dims):
    ah, al = split2(a)
    bh, bl = split2(b)
    return mm(ah, bh, dims) + (mm(ah, bl, dims) + mm(al, bh, dims))


def sigmoid(x):
    return 1.0 / (1.0 + jnp.exp(-x))


def lanes(value, q):
    return value[:, q * ATOMS : (q + 1) * ATOMS]


def plan(sizes):
    counts = [2 if s == 2 else 3 for s in sizes]
    moves = []
    for code in itertools.product(*[range(c) for c in counts]):
        moves.append(tuple({0: 0, 1: 1, 2: s - 1}[c] for c, s in zip(code, sizes)))
    return counts, moves[:0:-1]


def kernel(
    sizes,
    pos_any, spec_any, count_any, bound_any, send_any, ncount_any,
    emb_any, w1_any, w2_any, mix_any, read_any,
    force_ref, energy_ref,
    geo, rimgeo, geoland, oh, rid, off, gsc, bsc, dbp, yref, geom,
    pre, rad, feat, msg, dens, inv, dd, dysum, dbsum, dg, dr, ddsc, empad,
    rimh, hland, gland, dtab, gtab, cland, ex, ey, ez, etile,
    pos_ref, spec_ref, count_ref, bound_ref, send_ref, ncount_ref,
    emb_ref, w1_ref, w2_ref, mix_ref, read_ref, in_s,
    geo_s, geo_r, h_s, h_r, g_s, g_r, c_s, c_r, ex_s, ex_r, ey_s, ey_r, ez_s, ez_r,
):
    counts, moves = plan(sizes)
    D = len(moves)
    K = oh.shape[1]
    loads = {}
    for index, (name, src, dst) in enumerate((
        ("bound", bound_any, bound_ref), ("pos", pos_any, pos_ref), ("spec", spec_any, spec_ref),
        ("send", send_any, send_ref), ("ncount", ncount_any, ncount_ref), ("count", count_any, count_ref),
        ("emb", emb_any, emb_ref), ("w1", w1_any, w1_ref), ("w2", w2_any, w2_ref),
        ("read", read_any, read_ref), ("mix", mix_any, mix_ref),
    )):
        loads[name] = pltpu.make_async_copy(src, dst, in_s.at[index])
        loads[name].start()
    me = [lax.axis_index(a) for a in AXES]

    def at(move, sign):
        return {
            a: lax.rem(m + (d if sign > 0 else s - d), s)
            for a, m, d, s in zip(AXES, me, move, sizes)
        }

    def remote(src, dst, s_sem, r_sem, where):
        return pltpu.make_async_remote_copy(
            src_ref=src, dst_ref=dst, send_sem=s_sem, recv_sem=r_sem,
            device_id=where, device_id_type=pl.DeviceIdType.MESH,
        )

    spare = hland.shape[0] - D * RIM
    if spare:
        hland[D * RIM :, :] = jnp.zeros((spare, CH), F32)
        gland[D * RIM :, :] = jnp.zeros((spare, CH), F32)

    partners = list(moves)
    for axis, s in enumerate(sizes):
        for d in range(1, s):
            move = tuple(d if i == axis else 0 for i in range(3))
            if move not in partners:
                partners.append(move)
    barrier = pltpu.get_barrier_semaphore()
    for move in partners:
        pl.semaphore_signal(barrier, inc=1, device_id=at(move, 1), device_id_type=pl.DeviceIdType.MESH)

    for name in ("bound", "pos", "spec"):
        loads[name].wait()
    brow = bound_ref[0, 0]
    brow = jnp.concatenate([brow] * 4, axis=1)
    atom_row = lax.broadcasted_iota(jnp.int32, (ATOMS, ATOMS), 0)
    pick = (atom_row == brow).astype(F32)
    pick_t = pick.T
    coords = pos_ref[0, 0, :, 0, :]
    kinds = spec_ref[0, 0].astype(F32)
    geo[...] = jnp.zeros_like(geo)
    geo[0:3, :] = coords
    geo[3:4, :] = kinds
    own_geo = geo[...]
    g0, g1, g2 = split3(own_geo)
    rimgeo[...] = (mm(g0, pick, NN) + mm(g1, pick, NN)) + mm(g2, pick, NN)

    pl.semaphore_wait(barrier, len(partners))
    geo_copies = [
        remote(rimgeo, geoland.at[j], geo_s.at[j], geo_r.at[j], at(moves[j], -1)) for j in range(D)
    ]
    for c in geo_copies:
        c.start()

    for name in ("send", "ncount"):
        loads[name].wait()
    s = send_ref[0, 0, 0]
    slot_index = lax.broadcasted_iota(jnp.int32, (NEIGH, ATOMS), 0)
    live = slot_index < ncount_ref[0, 0]
    ghost = s >= ATOMS
    t = jnp.where(ghost, s - ATOMS, 0)
    slot = lax.shift_right_logical(t, 5)
    row = t - slot * RIM
    one = lambda c: jnp.where(c, 1, 0)
    sx = one(slot >= 9) + one(slot >= 18)
    rem = slot - 9 * sx
    sy = one(rem >= 3) + one(rem >= 6)
    sz = rem - 3 * sy
    ident = jnp.zeros_like(s)
    for axis, (v, cnt) in enumerate(zip((sx, sy, sz), counts)):
        code = one(v != 1) if cnt == 2 else jnp.where(v == 0, 2, v - 1)
        ident = ident * cnt + code
        off[axis] = jnp.where(ghost, (v - 1).astype(F32), 0.0)
    rows = jnp.where(ghost, ATOMS + (D - ident) * RIM + row, s)
    rid[...] = jnp.where(live, rows, -1)

    table_row = lax.broadcasted_iota(jnp.int32, (K, ATOMS), 0)

    def build(i, carry):
        for q in range(GROUP):
            r = rid[pl.ds(i * GROUP + q, 1), :]
            oh[i, :, q * ATOMS : (q + 1) * ATOMS] = jnp.where(table_row == r, 1.0, 0.0).astype(BF16)
        return carry

    lax.fori_loop(0, STEPS, build, 0, unroll=UNROLL)

    for name in ("emb", "w1", "w2", "count", "read", "mix"):
        loads[name].wait()
    empad[...] = jnp.zeros_like(empad)
    empad[0:NSPEC, :] = emb_ref[...]
    eh, el = split2(empad[...])
    emb_cat = jnp.concatenate([eh, el], axis=0)
    spec_row = lax.broadcasted_iota(jnp.int32, (32, ATOMS), 0)
    spec_row = jnp.where(spec_row >= 16, spec_row - 16, spec_row).astype(F32)
    h0 = mm(emb_cat, (spec_row == kinds).astype(F32), TN)
    ddsc[...] = jnp.zeros_like(ddsc)
    readout = jnp.broadcast_to(read_ref[...], (ATOMS, CH)).T
    live_atoms = (
        lax.broadcasted_iota(jnp.int32, (CH, ATOMS), 1) < count_ref[0, 0]
    ).astype(F32)

    for c in geo_copies:
        c.wait()
    lane_block = lax.shift_right_logical(lax.broadcasted_iota(jnp.int32, (8, ATOMS), 1), 5)
    tiles = [own_geo]
    for tile in range(K // ATOMS - 1):
        value = jnp.zeros((8, ATOMS), F32)
        for b in range(4):
            if tile * 4 + b < D:
                value = jnp.where(lane_block == b, geoland[tile * 4 + b], value)
        tiles.append(value)
    table_geo = jnp.concatenate(split3(jnp.concatenate(tiles, axis=1)), axis=0).astype(BF16)

    def gather_geo(i, carry):
        x = lax.dot_general(table_geo, oh[i], NN, preferred_element_type=F32)
        x = (x[0:8] + x[8:16]) + x[16:24]
        for q in range(GROUP):
            gsc[i * GROUP + q] = lanes(x, q)
        return carry

    lax.fori_loop(0, STEPS, gather_geo, 0, unroll=UNROLL)

    deltas = [(gsc[:, a, :] + off[a]) - coords[a : a + 1, :] for a in range(3)]
    dist = jnp.sqrt(deltas[0] * deltas[0] + deltas[1] * deltas[1] + deltas[2] * deltas[2] + 0.25)
    rinv = 1.0 / dist
    ux, uy, uz = (d * rinv for d in deltas)
    geom[0], geom[1], geom[2], geom[3] = ux, uy, uz, rinv
    ylm = [
        None, R3 * ux, R3 * uy, R3 * uz,
        R15 * ux * uy, R15 * uy * uz, R15 * uz * ux,
        (0.5 * R15) * (ux * ux - uy * uy), (0.5 * R5) * (3.0 * uz * uz - 1.0),
    ]
    for k in range(1, 9):
        yref[k] = ylm[k]
    q4 = dist * 0.25
    inner = 1.0 - q4 * q4
    env = inner * inner * rinv
    denv = -(inner * q4 + env) * rinv
    s1, c1 = jnp.sin(PI * q4), jnp.cos(PI * q4)
    sm, cm, sp, cp = s1, c1, jnp.zeros_like(s1), jnp.ones_like(s1)
    for m in range(NB):
        bsc[:, m, :] = sm * env
        dbp[m] = ((m + 1) * PI * 0.25) * cm * env + sm * denv
        sm, sp = 2.0 * c1 * sm - sp, sm
        cm, cp = 2.0 * c1 * cm - cp, cm
    kind_edge = gsc[:, 3, :]
    rid_kind = jnp.where(live, kind_edge, -1.0)
    geom[4] = rid_kind

    def radial(layer, with_feat):
        w1h, w1l = split2(w1_ref[layer])
        w1c = jnp.concatenate([w1h, w1h, w1l], axis=0).astype(BF16)
        w2h, w2l = split2(w2_ref[layer])
        w2c = jnp.concatenate([w2h, w2h, w2l], axis=0).astype(BF16)

        def step(i, carry):
            b = jnp.concatenate([bsc[i * GROUP + q] for q in range(GROUP)], axis=1)
            bh, bl = split2(b)
            bc = jnp.concatenate([bh, bl, bh], axis=0).astype(BF16)
            p = lax.dot_general(w1c, bc, TN, preferred_element_type=F32)
            pre[layer, i] = p
            hid = p * sigmoid(p)
            hh, hl = split2(hid)
            hc = jnp.concatenate([hh, hl, hh], axis=0).astype(BF16)
            r = lax.dot_general(w2c, hc, TN, preferred_element_type=F32)
            rad[i] = r
            if with_feat:
                for q in range(GROUP):
                    kind = geom[4, pl.ds(i * GROUP + q, 1), :]
                    f = mm(emb_cat, (spec_row == kind).astype(F32), TN)
                    feat[layer, i, :, q * ATOMS : (q + 1) * ATOMS] = f
                    msg[layer, i, :, q * ATOMS : (q + 1) * ATOMS] = f * lanes(r, q)
            return carry

        lax.fori_loop(0, STEPS, step, 0, unroll=UNROLL)

    def density(layer):
        def step(cb, carry):
            at_rows = pl.ds(pl.multiple_of(cb * 16, 16), 16)
            acc = [None] * 9
            for n in range(NEIGH):
                lo = (n % GROUP) * ATOMS
                m = msg[layer, n // GROUP, at_rows, lo : lo + ATOMS]
                for k in range(9):
                    term = m if k == 0 else m * yref[k, n : n + 1, :]
                    acc[k] = term if n == 0 else acc[k] + term
            acc = [a * (1.0 / NEIGH) for a in acc]
            for k in range(9):
                dens[k, at_rows, :] = acc[k]
            inv[0, at_rows, :] = acc[0]
            inv[1, at_rows, :] = acc[1] * acc[1] + acc[2] * acc[2] + acc[3] * acc[3]
            sq = acc[4] * acc[4]
            for k in range(5, 9):
                sq = sq + acc[k] * acc[k]
            inv[2, at_rows, :] = sq
            return carry

        lax.fori_loop(0, CH // 16, step, 0)
        z = None
        for part in range(3):
            term = dot3(mix_ref[layer, part * CH : (part + 1) * CH, :], inv[part], TN)
            z = term if z is None else z + term
        return z

    def density_grad(layer, dz):
        for part in range(3):
            d = dot3(mix_ref[layer, part * CH : (part + 1) * CH, :], dz, NN)
            if part == 0:
                dd[0] = d * (1.0 / NEIGH)
            else:
                d = d * (2.0 / NEIGH)
                for k in range(1, 4) if part == 1 else range(4, 9):
                    dd[k] = d * dens[k]

    radial(0, True)
    z1 = density(0)
    sig1 = sigmoid(z1)
    h1 = h0 + z1 * sig1
    dz1 = sig1 * (1.0 + z1 * (1.0 - sig1))
    first = [dens[k] for k in range(1, 9)]
    for k in range(1, 9):
        dd[9 + k] = first[k - 1]

    hh, hl = split2(h1)
    rimh[...] = mm(pick_t[0:RIM], hh, NT) + mm(pick_t[0:RIM], hl, NT)
    h_copies = [
        remote(rimh, hland.at[pl.ds(j * RIM, RIM)], h_s.at[j], h_r.at[j], at(moves[j], -1))
        for j in range(D)
    ]
    for c in h_copies:
        c.start()
    radial(1, False)
    for c in h_copies:
        c.wait()

    parts_t = [h1] + [hland[u * ATOMS : (u + 1) * ATOMS, :].T for u in range(K // ATOMS - 1)]
    table_h = jnp.concatenate(split2(jnp.concatenate(parts_t, axis=1)), axis=0).astype(BF16)

    def gather_h(i, carry):
        x = lax.dot_general(table_h, oh[i], NN, preferred_element_type=F32)
        f = x[0:CH] + x[CH : 2 * CH]
        feat[1, i] = f
        msg[1, i] = f * rad[i]
        return carry

    lax.fori_loop(0, STEPS, gather_h, 0, unroll=UNROLL)
    z2 = density(1)
    sig2 = sigmoid(z2)
    final = h1 + z2 * sig2
    sigf = sigmoid(final)
    weight = readout * live_atoms
    contrib = weight * (final * sigf)
    part = contrib[0:8]
    for u in range(1, CH // 8):
        part = part + contrib[u * 8 : (u + 1) * 8]

    def spread(axis, land, s_sem, r_sem, value):
        size = sizes[axis]
        mine = me[axis]
        land[mine] = value
        copies = []
        for d in range(1, size):
            move = tuple(d if i == axis else 0 for i in range(3))
            copies.append(remote(land.at[mine], land.at[mine], s_sem.at[d], r_sem.at[d], at(move, 1)))
        for c in copies:
            c.start()
        return copies

    def gathered(axis, land, copies):
        for c in copies:
            c.wait()
        total = land[0]
        for i in range(1, sizes[axis]):
            total = total + land[i]
        return total

    e_copies = spread(0, ex, ex_s, ex_r, part)

    dfinal = weight * (sigf * (1.0 + final * (1.0 - sigf)))
    density_grad(1, dfinal * (sig2 * (1.0 + z2 * (1.0 - sig2))))

    def back_feat(i, carry):
        for q in range(GROUP):
            cut = slice(q * ATOMS, (q + 1) * ATOMS)
            dm = dd[0]
            for k in range(1, 9):
                dm = dm + yref[k, pl.ds(i * GROUP + q, 1), :] * dd[k]
            gh, gl = split2(dm * rad[i, :, cut])
            dg[i, 0:CH, cut] = gh.astype(BF16)
            dg[i, CH : 2 * CH, cut] = gl.astype(BF16)
            dr[i, :, cut] = dm * feat[1, i, :, cut]
        return carry

    lax.fori_loop(0, STEPS, back_feat, 0, unroll=UNROLL)

    dtab[...] = jnp.zeros_like(dtab)

    def scatter_h(i, carry):
        dtab[...] += lax.dot_general(oh[i], dg[i], NT, preferred_element_type=F32)
        return carry

    lax.fori_loop(0, STEPS, scatter_h, 0, unroll=UNROLL)
    gtab[...] = dtab[:, 0:CH] + dtab[:, CH : 2 * CH]
    g_copies = [
        remote(
            gtab.at[pl.ds(ATOMS + j * RIM, RIM)], gland.at[pl.ds(j * RIM, RIM)],
            g_s.at[j], g_r.at[j], at(moves[j], 1),
        )
        for j in range(D)
    ]
    for c in g_copies:
        c.start()
    own_dh = gtab[0:ATOMS, :].T

    def back_radial(layer, first_pass):
        w1h, w1l = split2(w1_ref[layer])
        w2h, w2l = split2(w2_ref[layer])
        w2c = jnp.concatenate([w2h, w2h, w2l], axis=1).astype(BF16)

        def step(i, carry):
            v = dr[i]
            vh, vl = split2(v)
            vc = jnp.concatenate([vh, vl, vh], axis=0).astype(BF16)
            dhid = lax.dot_general(w2c, vc, NN, preferred_element_type=F32)
            p = pre[layer, i]
            sg = sigmoid(p)
            dp = dhid * (sg * (1.0 + p * (1.0 - sg)))
            ph, p_lo = split2(dp)
            db = mm(w1h, ph, NN) + (mm(w1h, p_lo, NN) + mm(w1l, ph, NN))
            for q in range(GROUP):
                if first_pass:
                    dbsum[i * GROUP + q] = lanes(db, q)
                else:
                    dbsum[i * GROUP + q] += lanes(db, q)
            return carry

        lax.fori_loop(0, STEPS, step, 0, unroll=UNROLL)

    def back_sphere(i, carry):
        for q in range(GROUP):
            cut = slice(q * ATOMS, (q + 1) * ATOMS)
            m = msg[1, i, :, cut]
            for k in range(1, 9):
                dysum[k, pl.ds(i * GROUP + q, 1), :] = jnp.sum(m * dd[k], axis=0, keepdims=True)
        return carry

    lax.fori_loop(0, STEPS, back_sphere, 0, unroll=UNROLL)
    back_radial(1, True)
    part = gathered(0, ex, e_copies)
    e_copies = spread(1, ey, ey_s, ey_r, part)

    for c in g_copies:
        c.wait()
    back = gland[0:ATOMS, :]
    for u in range(1, gland.shape[0] // ATOMS):
        back = back + gland[u * ATOMS : (u + 1) * ATOMS, :]
    bh, bl = split2(back.T)
    dh1 = dfinal + own_dh + (mm(bh, pick, NT) + mm(bl, pick, NT))
    for k in range(1, 9):
        dens[k] = dd[9 + k]
    density_grad(0, dh1 * dz1)

    def back_first(i, carry):
        for q in range(GROUP):
            cut = slice(q * ATOMS, (q + 1) * ATOMS)
            m = msg[0, i, :, cut]
            dm = dd[0]
            for k in range(1, 9):
                at_n = pl.ds(i * GROUP + q, 1)
                g = dd[k]
                dm = dm + yref[k, at_n, :] * g
                dysum[k, at_n, :] += jnp.sum(m * g, axis=0, keepdims=True)
            dr[i, :, cut] = dm * feat[0, i, :, cut]
        return carry

    lax.fori_loop(0, STEPS, back_first, 0, unroll=UNROLL)
    back_radial(0, False)
    part = gathered(1, ey, e_copies)
    e_copies = spread(2, ez, ez_s, ez_r, part)

    ux, uy, uz, rinv = geom[0], geom[1], geom[2], geom[3]
    dy = [None] + [dysum[k] for k in range(1, 9)]
    gx = R3 * dy[1] + R15 * (uy * dy[4] + uz * dy[6] + ux * dy[7])
    gy = R3 * dy[2] + R15 * (ux * dy[4] + uz * dy[5] - uy * dy[7])
    gz = R3 * dy[3] + R15 * (uy * dy[5] + ux * dy[6]) + (3.0 * R5) * uz * dy[8]
    drad = dbsum[:, 0, :] * dbp[0]
    for m in range(1, NB):
        drad = drad + dbsum[:, m, :] * dbp[m]
    drad = drad - (gx * ux + gy * uy + gz * uz) * rinv
    centre = []
    for a, (g, u) in enumerate(((gx, ux), (gy, uy), (gz, uz))):
        d = jnp.where(live, g * rinv + u * drad, 0.0)
        ddsc[:, a, :] = d
        centre.append(jnp.sum(d, axis=0, keepdims=True))

    def scatter_geo(i, carry):
        d = jnp.concatenate([ddsc[i * GROUP + q] for q in range(GROUP)], axis=1)
        d = jnp.concatenate(split2(d), axis=0).astype(BF16)
        return carry + lax.dot_general(d, oh[i], NT, preferred_element_type=F32)

    dxyz = lax.fori_loop(0, STEPS, scatter_geo, jnp.zeros((16, K), F32), unroll=UNROLL)
    dxyz = dxyz[0:8] + dxyz[8:16]
    for u in range(K // ATOMS):
        etile[u] = lanes(dxyz, u)
    c_copies = [
        remote(etile.at[1 + j // 4], cland.at[j], c_s.at[j], c_r.at[j], at(moves[j], 1))
        for j in range(D)
    ]
    for c in c_copies:
        c.start()
    part = gathered(2, ez, e_copies)
    slots = float(ATOMS * sizes[0] * sizes[1] * sizes[2])
    energy_ref[...] = jnp.broadcast_to(jnp.sum(part) / slots, energy_ref.shape)
    for c in c_copies:
        c.wait()
    ret = jnp.zeros((8, ATOMS), F32)
    for j in range(D):
        ret = ret + jnp.where(lane_block == j % 4, cland[j], 0.0)
    r0, r1 = split2(ret)
    grad = etile[0] + (mm(r0, pick, NT) + mm(r1, pick, NT))
    for a in range(3):
        force_ref[0, 0, a] = centre[a] - grad[a : a + 1, :]


def on_device(
    sizes, positions, species, atom_count, boundary, senders, neighbour_count,
    embed, radial_first, radial_second, mix, readout,
):
    _, moves = plan(sizes)
    D = len(moves)
    T = -(-D * RIM // ATOMS)
    K = ATOMS * (1 + T)
    vm = pltpu.VMEM
    dma = pltpu.SemaphoreType.DMA
    scratch = [
        vm((8, ATOMS), F32),
        vm((8, ATOMS), F32),
        vm((D, 8, ATOMS), F32),
        vm((STEPS, K, WIDE), BF16),
        vm((NEIGH, ATOMS), jnp.int32),
        vm((3, NEIGH, ATOMS), F32),
        vm((NEIGH, 8, ATOMS), F32),
        vm((NEIGH, NB, ATOMS), F32),
        vm((NB, NEIGH, ATOMS), F32),
        vm((9, NEIGH, ATOMS), F32),
        vm((5, NEIGH, ATOMS), F32),
        vm((2, STEPS, RH, WIDE), F32),
        vm((STEPS, CH, WIDE), F32),
        vm((2, STEPS, CH, WIDE), F32),
        vm((2, STEPS, CH, WIDE), F32),
        vm((9, CH, ATOMS), F32),
        vm((3, CH, ATOMS), F32),
        vm((18, CH, ATOMS), F32),
        vm((9, NEIGH, ATOMS), F32),
        vm((NEIGH, NB, ATOMS), F32),
        vm((STEPS, 2 * CH, WIDE), BF16),
        vm((STEPS, CH, WIDE), F32),
        vm((NEIGH, 8, ATOMS), F32),
        vm((16, CH), F32),
        vm((RIM, CH), F32),
        vm((T * ATOMS, CH), F32),
        vm((T * ATOMS, CH), F32),
        vm((K, 2 * CH), F32),
        vm((K, CH), F32),
        vm((D, 8, ATOMS), F32),
        vm((sizes[0], 8, ATOMS), F32),
        vm((sizes[1], 8, ATOMS), F32),
        vm((sizes[2], 8, ATOMS), F32),
        vm((1 + T, 8, ATOMS), F32),
    ]
    operands = (
        positions.reshape(1, 1, 3, 1, ATOMS), species.reshape(1, 1, 1, ATOMS), atom_count.reshape(1, 1, 1, 1),
        boundary.reshape(1, 1, 1, RIM), senders, neighbour_count.reshape(1, 1, 1, ATOMS),
        embed, radial_first, radial_second, mix, readout.reshape(1, CH),
    )
    scratch += [vm(x.shape, x.dtype) for x in operands] + [dma((len(operands),))]
    for amount in (D, D, D, D, sizes[0], sizes[1], sizes[2]):
        scratch += [dma((amount,)), dma((amount,))]
    forces, energy = pl.pallas_call(
        functools.partial(kernel, sizes),
        out_shape=(
            jax.ShapeDtypeStruct((1, 1, 3, 1, ATOMS), F32),
            jax.ShapeDtypeStruct((1, ATOMS), F32),
        ),
        in_specs=[pl.BlockSpec(memory_space=pltpu.HBM)] * 11,
        out_specs=(pl.BlockSpec(memory_space=pltpu.VMEM),) * 2,
        scratch_shapes=scratch,
        compiler_params=pltpu.CompilerParams(
            collective_id=0, has_side_effects=True, vmem_limit_bytes=VMEM_BYTES
        ),
        name="brick",
    )(*operands)
    return forces.reshape(positions.shape), energy[0, 0:1]


def solution(mesh):
    sizes = tuple(mesh.shape[a] for a in AXES)
    brick = lambda extra: P(("groups", "gx"), "gy", "gz", *([None] * extra))
    in_specs = (brick(2), brick(1), brick(1), brick(1), brick(2), brick(1), P(), P(), P(), P(), P())
    return jax.shard_map(
        functools.partial(on_device, sizes),
        mesh=mesh,
        in_specs=in_specs,
        out_specs=(brick(2), P("groups")),
        check_vma=False,
    )
```
